32 devices in a mesh: rows: 4 (over z), nodes: 8 (over y, x, core).
Axes of the slice: x: 2, y: 2, z: 4, core: 2. Of those that a mesh axis runs over, the one named last changes fastest.
Arguments:
- codes: int32 [65536, 128], P('rows'), may hold values from 0 to 16367
- sample_idx: int32 [32768], P(('rows', 'nodes')), may hold values from 0 to 16383, as said below
- node_of_row: int32 [32768, 1], P(('rows', 'nodes')), may hold values from 0 to 63; in each aligned block of 1024 rows (0 to 1023, 1024 to 2047, ...) at most 48 rows name the same one
- small_flag: int32 [32768], P(('rows', 'nodes')), may hold values 0 or 1
- preds: bfloat16 [16, 32768], P(None, ('rows', 'nodes')), may hold values from -6 to 6
- targets: float32 [32768], P(('rows', 'nodes')), may hold values from -6 to 6
Outputs:
- best_gain: float32 [64, 256], P('nodes', 'rows')
The draws below stay inside these ranges and needn't reach their ends.
Inputs may be any that keep to these rules, and one draw needn't show every extreme that they name: `node_of_row`: in each aligned block of 1024 rows (the rows of one device) no node is named by more than 48 rows, a bound that some block reaches. `sample_idx`: distinct within each aligned block of 8192 rows.
All inputs are finite; a program needn't handle non-finite values. No bound on the sum of `small_flag` on one device may be relied on, other than what follows from the above.
Results may differ from the reference program's by a relative error of at most 0.00099.
Values may be sent and summed in bfloat16 or wider, within the bound.
A program may use at most 128 MiB of HBM per device.

```python
import math
import jax
import jax.numpy as jnp
import numpy as np
from jax import lax

FEATS = 256
BINS = 128
QUANT = 16
ROW_DEV = 1024
CAP = 48
NODES = 64
POOL_BLK = 16384
ROWS = 32768
N_ROWS = 4
N_NODES = 8


def draw_sample_idx(key, part):
    key = jax.random.fold_in(key, 11)
    keys = jax.random.split(key, N_ROWS)

    def one_block(block_key):
        order = jax.random.permutation(block_key, POOL_BLK).astype(jnp.int32)[:N_NODES * ROW_DEV]
        highest = jnp.max(order)
        return jnp.where(order == highest, POOL_BLK - 1, order).astype(jnp.int32)
    return jax.vmap(one_block)(keys).reshape(-1)


def touch_ends(values, stream_key, smallest, top_value):
    index_at = [jax.random.randint(jax.random.fold_in(stream_key, axis), (), 0, length) for axis, length in enumerate(values.shape)]
    main_axis = values.shape.index(max(values.shape))
    beside = index_at[:main_axis] + [(index_at[main_axis] + 1) % values.shape[main_axis]] + index_at[main_axis + 1:]
    return values.at[tuple(index_at)].set(smallest).at[tuple(beside)].set(top_value)


def level_of(own_key, shape, shards, low, high):
    def one(position, shards_of):
        draws = jax.random.uniform(jax.random.fold_in(jax.random.fold_in(own_key, 6), position), (shards_of,), jnp.float32, low / len(shards), high / len(shards))
        return jnp.repeat(jnp.exp(draws), shape[position] // shards_of).reshape((-1,) + (1,) * (len(shape) - position - 1))

    level = one(*shards[0])
    for cut in shards[1:]:
        level = level * one(*cut)
    return level


def shared_out(stream_key, own, number, rows, number_of, top, most, skew):
    sequence = jax.random.permutation(stream_key, number_of)
    heavy_load, common = portions_of(number_of, rows * top, most, skew, True), portions_of(number_of, rows * top, most, skew, False)
    places = jnp.arange(number_of)

    def named(lengths, turn):
        used = int((lengths > 0).sum())
        fixed = max(1, used // 4)
        moved = fixed + (places - fixed + turn * (used - fixed)) % max(1, number_of - fixed)
        return jnp.zeros((number_of,), jnp.int32).at[sequence[jnp.where(places < fixed, places, moved)]].set(jnp.asarray(lengths, jnp.int32))

    lengths = jnp.where(number % 4 == 0, named(heavy_load, number // 4), named(common, number - number // 4 - 1))
    mixed = jax.random.permutation(jax.random.fold_in(own, 3), number_of)
    source_of, taker = mixed[0:number_of // 2 * 2:2], mixed[1:number_of // 2 * 2:2]
    margin = jnp.minimum(lengths[source_of] - 1, most - lengths[taker]) // 2
    margin = jnp.where((source_of == sequence[0]) | (taker == sequence[0]) | (lengths[taker] == 0), 0, jnp.maximum(margin, 0))
    moved = jax.random.randint(jax.random.fold_in(own, 4), (number_of // 2,), 0, 1 << 20) % (margin + 1)
    lengths = lengths.at[source_of].add(-moved).at[taker].add(moved)
    items = jnp.searchsorted(jnp.cumsum(lengths), jnp.arange(rows * top), side="right").astype(jnp.int32)
    listing = items.reshape(top, rows).T
    listing = listing[jax.random.permutation(jax.random.fold_in(own, 1), rows)]
    turn = jax.random.randint(jax.random.fold_in(own, 2), (rows, 1), 0, top)
    return jnp.take_along_axis(listing, (jnp.arange(top)[None, :] + turn) % top, axis=1)


def portions_of(count, total, limit, lean, full):
    portions = [(1 << 20) // math.isqrt(standing ** lean) + 1 for standing in range(1, count + 1)]
    largest = limit if full else min(limit, max(-(-total // count), total * portions[0] // sum(portions)))
    least = 1 if total - largest >= count - 1 else 0
    holding, surplus = [largest] + [least] * (count - 1), total - largest - least * (count - 1)
    while surplus > 0:
        movable = [i for i in range(1, count) if holding[i] < largest] or [i for i in range(1, count) if holding[i] < limit]
        pool, remaining = sum([portions[i] for i in movable]), surplus
        for i in movable:
            extra = min(limit - holding[i], max(1, remaining * portions[i] // pool), surplus)
            holding[i] = holding[i] + extra
            surplus = surplus - extra
    return np.array(holding)


def centred(own_key, dims, scale, reach, cuts=(), kind=jnp.bfloat16):
    drawn = scale * jax.random.normal(own_key, dims, jnp.float32)
    if cuts:
        drawn = drawn * level_of(own_key, dims, cuts, -0.22, 0.18)
    return jnp.clip(drawn, -reach, reach).astype(kind)


def setup_inputs(seed: int = 0) -> dict:
    key_list = jax.random.split(jax.random.key(seed), 7)
    codes = touch_ends(jax.random.randint(key_list[0], (N_ROWS * POOL_BLK, FEATS // 2), 0, BINS ** 2 - 16), jax.random.fold_in(key_list[0], 1), 0, (BINS ** 2 - 16) - 1).astype(jnp.int32)
    sample_idx = draw_sample_idx(jax.random.fold_in(key_list[6], 71), 0)
    node_of_row_keys = jax.random.split(jax.random.fold_in(key_list[2], 1), ROWS // ROW_DEV)
    node_of_row_turns = jax.random.permutation(jax.random.fold_in(key_list[2], 3), ROWS // ROW_DEV)
    node_of_row = jax.vmap(lambda own, number: shared_out(jax.random.fold_in(key_list[2], 2), own, number, ROW_DEV, NODES, 1, CAP, 2))(node_of_row_keys, node_of_row_turns).reshape((ROWS, 1))
    small_flag = touch_ends((jax.random.randint(key_list[3], (ROWS,), 0, 3) < 1).astype(jnp.int32), jax.random.fold_in(key_list[3], 1), 0, 1)
    preds = centred(key_list[4], (QUANT, ROWS), 1.0, 6.0, ((1, 32),))
    targets = centred(key_list[5], (ROWS,), 1.0, 6.0, ((0, 32),), jnp.float32)
    return {"codes": codes, "sample_idx": sample_idx, "node_of_row": node_of_row, "small_flag": small_flag, "preds": preds, "targets": targets}


SMOOTH = 0.5
RIDGE = 1.0
BOOST = 8.0


def quantile_grads(preds, targets, small_flag):
    count = preds.shape[0]
    levels = (jnp.arange(count, dtype=jnp.float32) + 0.5) / count
    weight = 1.0 + (BOOST - 1.0) * small_flag.astype(jnp.float32)
    slope = jax.nn.sigmoid((preds.astype(jnp.float32) - targets[None, :]) / SMOOTH) - levels[:, None]
    return (slope * weight[None, :]).astype(jnp.bfloat16), weight.astype(jnp.bfloat16)[None, :]


def split_gain(hist):
    quant = hist.shape[-2] - 1
    left = jnp.cumsum(hist, axis=-1)
    total = left[..., -1:]
    grad_left = left[..., :quant, :-1]
    hess_left = left[..., quant:, :-1]
    grad_all = total[..., :quant, :]
    hess_all = total[..., quant:, :]
    grad_right = grad_all - grad_left
    hess_right = hess_all - hess_left
    score = grad_left * grad_left / (hess_left + RIDGE) + grad_right * grad_right / (hess_right + RIDGE) - grad_all * grad_all / (hess_all + RIDGE)
    return jnp.max(jnp.sum(score, axis=-2), axis=-1) / quant


def reference(codes, sample_idx, node_of_row, small_flag, preds, targets):
    total_rows = sample_idx.shape[0]
    block = jnp.arange(total_rows, dtype=jnp.int32) // (N_NODES * ROW_DEV)
    rows_at = (block * POOL_BLK + sample_idx).astype(jnp.int32)
    words = codes[rows_at]
    slopes, weight = quantile_grads(preds, targets, small_flag)
    channels = jnp.concatenate([slopes, weight], axis=0).astype(jnp.float32).T
    node = node_of_row[:, 0]
    powers = (BINS ** jnp.arange(2, dtype=jnp.int32)).astype(jnp.int32)

    def one_feature(feature):
        column = lax.dynamic_index_in_dim(words, (feature // 2).astype(jnp.int32), 1, keepdims=False)
        power = lax.dynamic_index_in_dim(powers, (feature % 2).astype(jnp.int32), 0, keepdims=False)
        binned = (column // power) % BINS
        summed = jax.ops.segment_sum(channels, (node * BINS + binned).astype(jnp.int32), num_segments=NODES * BINS)
        return summed.reshape(NODES, BINS, -1).transpose(0, 2, 1)

    hist = lax.map(one_feature, jnp.arange(FEATS, dtype=jnp.int32))
    return split_gain(hist).T
```

```python
import functools

import jax
import jax.numpy as jnp
from jax import lax
from jax.experimental import pallas as pl
from jax.experimental.pallas import tpu as pltpu
from jax.sharding import PartitionSpec as P

BINS = 128
CAP = 48
TOTAL_NODES = 64
SMOOTH = 0.5
RIDGE = 1.0
BOOST = 8.0
CHANS = 32
TILE = 128
STEP = 4
NT = (((1,), (1,)), ((), ()))
VMEM = pl.BlockSpec(memory_space=pltpu.VMEM)
SMEM = pl.BlockSpec(memory_space=pltpu.SMEM)


def pack_kernel(preds_ref, targets_ref, flag_ref, index_ref, node_ref, out_ref):
    quant, rows = preds_ref.shape
    groups, _, slots = out_ref.shape
    node_grp = TOTAL_NODES // groups
    levels = (lax.broadcasted_iota(jnp.int32, (quant, 1), 0).astype(jnp.float32) + 0.5) / quant
    weight = 1.0 + (BOOST - 1.0) * flag_ref[...].astype(jnp.float32)
    gap = (preds_ref[...].astype(jnp.float32) - targets_ref[...]) / SMOOTH
    slopes = (1.0 / (1.0 + jnp.exp(-gap)) - levels) * weight
    node = node_ref[...]
    group = node // node_grp
    place = index_ref[...]
    rest = [weight, (node - group * node_grp).astype(jnp.float32), (place // 128).astype(jnp.float32), (place % 128).astype(jnp.float32)]
    vals = jnp.concatenate(
        [slopes] + rest + [jnp.zeros((CHANS - quant - len(rest), rows), jnp.float32)], axis=0
    ).astype(jnp.bfloat16)
    own = (lax.broadcasted_iota(jnp.int32, (groups, rows), 0) == group).astype(jnp.float32)
    upto = (
        lax.broadcasted_iota(jnp.int32, (rows, rows), 0) <= lax.broadcasted_iota(jnp.int32, (rows, rows), 1)
    ).astype(jnp.float32)
    run = jnp.dot(own.astype(jnp.bfloat16), upto.astype(jnp.bfloat16), preferred_element_type=jnp.float32)
    rank = jnp.sum(run * own, axis=0, keepdims=True).astype(jnp.int32) - 1
    slot = lax.broadcasted_iota(jnp.int32, (slots, rows), 0)
    for g in range(groups):
        pick = (slot == jnp.where(group == g, rank, -1)).astype(jnp.float32).astype(jnp.bfloat16)
        out_ref[g] = lax.dot_general(vals, pick, NT, preferred_element_type=jnp.float32).astype(jnp.bfloat16)


def gain_kernel(quant, count_ref, chan_ref, word_ref, out_ref, list_ref, left_ref, tile_ref, acc_ref):
    spread, groups, _, slots = chan_ref.shape
    words = word_ref.shape[1]
    node_grp = out_ref.shape[0]
    per = slots // TILE

    def fill(pair, used):
        have = count_ref[pair]
        for s in range(per):
            live = have > s * TILE
            list_ref[used] = pair * per + s
            used = used + live.astype(jnp.int32)
        return used

    used = lax.fori_loop(0, spread * groups, fill, jnp.int32(0))
    for u in range(STEP):
        list_ref[used + u] = -1
    acc_ref[...] = jnp.zeros_like(acc_ref)
    kinds = lax.broadcasted_iota(jnp.int32, (node_grp, TILE), 0).astype(jnp.float32)
    level = lax.broadcasted_iota(jnp.int32, (BINS, STEP * TILE), 0).astype(jnp.float32).astype(jnp.bfloat16)

    def step(j, carry):
        for u in range(STEP):
            entry = list_ref[j * STEP + u]
            tile = jnp.maximum(entry, 0)
            pair = tile // per
            z, src = pair // groups, pair % groups
            s = tile % per
            part = chan_ref[z, src, :, pl.ds(pl.multiple_of(s * TILE, TILE), TILE)].astype(jnp.float32)
            mask = jnp.where((part[quant + 1:quant + 2] == kinds) & (entry >= 0), 1.0, 0.0)
            for c in range(quant + 1):
                left_ref[c * node_grp:(c + 1) * node_grp, u * TILE:(u + 1) * TILE] = part[c:c + 1] * mask
            tile_ref[u] = word_ref[z, :, pl.ds(pl.multiple_of((src * per + s) * TILE, TILE), TILE)]
        left = left_ref[...].astype(jnp.bfloat16)

        def feature(w, carry):
            row = jnp.concatenate([tile_ref[u, pl.ds(w, 1), :] for u in range(STEP)], axis=1)
            row = jnp.broadcast_to(row, (16, STEP * TILE))
            sides = []
            for digit in (row & (BINS - 1), row >> 7):
                digit = digit.astype(jnp.float32).astype(jnp.bfloat16)
                digit = jnp.broadcast_to(digit[None], (BINS // 16, 16, STEP * TILE)).reshape(BINS, STEP * TILE)
                sides.append(jnp.where(level >= digit, jnp.bfloat16(1), jnp.bfloat16(0)))
            side = jnp.concatenate(sides, axis=0)
            acc_ref[w] += lax.dot_general(left, side, NT, preferred_element_type=jnp.float32)
            return carry

        return lax.fori_loop(0, words, feature, carry, unroll=2)

    lax.fori_loop(0, (used + STEP - 1) // STEP, step, 0)

    lane = lax.broadcasted_iota(jnp.int32, out_ref.shape, 1)
    bins = lax.broadcasted_iota(jnp.int32, (node_grp, BINS), 1)

    def best_of(w, best):
        for c in range(2):
            sums = acc_ref[w, :, c * BINS:(c + 1) * BINS]
            hess = sums[quant * node_grp:]
            hess_all = hess[:, BINS - 1:]
            sq_left = sq_right = sq_all = 0.0
            for q in range(quant):
                grad = sums[q * node_grp:(q + 1) * node_grp]
                grad_all = grad[:, BINS - 1:]
                sq_left += grad * grad
                sq_right += (grad_all - grad) * (grad_all - grad)
                sq_all += grad_all * grad_all
            score = sq_left / (hess + RIDGE) + sq_right / (hess_all - hess + RIDGE) - sq_all / (hess_all + RIDGE)
            score = jnp.where(bins < BINS - 1, score, -jnp.inf)
            top = jnp.max(score, axis=1, keepdims=True) / quant
            best = jnp.where(lane == 2 * w + c, top, best)
        return best

    out_ref[...] = lax.fori_loop(0, words, best_of, jnp.zeros(out_ref.shape, jnp.float32))


def on_device(codes, sample_idx, node_of_row, small_flag, preds, targets):
    groups = lax.axis_size("nodes")
    spread = lax.axis_size("rows")
    quant, rows = preds.shape
    node_grp = TOTAL_NODES // groups
    slots = CAP * node_grp
    width = groups * slots
    share = codes.shape[1] // spread

    def line(x):
        return x.reshape(1, rows)

    packed = pl.pallas_call(
        pack_kernel,
        out_shape=jax.ShapeDtypeStruct((groups, CHANS, slots), jnp.bfloat16),
        in_specs=[VMEM] * 5,
        out_specs=VMEM,
        compiler_params=pltpu.CompilerParams(vmem_limit_bytes=40 << 20),
    )(preds, line(targets), line(small_flag), line(sample_idx), line(node_of_row))
    got = lax.all_to_all(packed, "nodes", split_axis=0, concat_axis=0, tiled=True)
    half = got[:, quant + 2:quant + 4, :].astype(jnp.int32)
    index = (half[:, 0] * 128 + half[:, 1]).reshape(width)
    lines = codes.at[index].get(mode="promise_in_bounds")
    words = lax.all_to_all(
        lines.T.reshape(spread, share, width), "rows", split_axis=0, concat_axis=0, tiled=True
    )
    chans = lax.all_gather(got, "rows")
    count = jnp.sum((chans[:, :, quant, :] > 0).astype(jnp.int32), axis=-1).reshape(-1)
    return pl.pallas_call(
        functools.partial(gain_kernel, quant),
        out_shape=jax.ShapeDtypeStruct((node_grp, 2 * share), jnp.float32),
        in_specs=[SMEM, VMEM, VMEM],
        out_specs=VMEM,
        scratch_shapes=[
            pltpu.SMEM((spread * groups * slots // TILE + 2 * STEP,), jnp.int32),
            pltpu.VMEM(((quant + 1) * node_grp, STEP * TILE), jnp.float32),
            pltpu.VMEM((STEP, share, TILE), jnp.int32),
            pltpu.VMEM((share, (quant + 1) * node_grp, 2 * BINS), jnp.float32),
        ],
        compiler_params=pltpu.CompilerParams(vmem_limit_bytes=48 << 20),
    )(count, chans, words)


def solution(mesh):
    return jax.shard_map(
        on_device,
        mesh=mesh,
        in_specs=(
            P("rows", None),
            P(("rows", "nodes")),
            P(("rows", "nodes"), None),
            P(("rows", "nodes")),
            P(None, ("rows", "nodes")),
            P(("rows", "nodes")),
        ),
        out_specs=P("nodes", "rows"),
        check_vma=False,
    )
```

```python
import functools

import jax
import jax.numpy as jnp
from jax import lax
from jax.experimental import pallas as pl
from jax.experimental.pallas import tpu as pltpu
from jax.sharding import PartitionSpec as P

BINS = 128
CAP = 48
TOTAL_NODES = 64
SMOOTH = 0.5
RIDGE = 1.0
BOOST = 8.0
CHANS = 32
TILE = 128
STEP = 4
NT = (((1,), (1,)), ((), ()))
VMEM = pl.BlockSpec(memory_space=pltpu.VMEM)
SMEM = pl.BlockSpec(memory_space=pltpu.SMEM)


def send_kernel(preds_ref, targets_ref, flag_ref, node_ref, line_ref, out_ref):
    quant, rows = preds_ref.shape
    spread, total, _ = out_ref.shape
    share = line_ref.shape[1] // spread
    levels = (lax.broadcasted_iota(jnp.int32, (quant, 1), 0).astype(jnp.float32) + 0.5) / quant
    weight = 1.0 + (BOOST - 1.0) * flag_ref[...].astype(jnp.float32)
    gap = (preds_ref[...].astype(jnp.float32) - targets_ref[...]) / SMOOTH
    slopes = (1.0 / (1.0 + jnp.exp(-gap)) - levels) * weight
    vals = jnp.concatenate(
        [slopes, weight, node_ref[...].astype(jnp.float32), jnp.zeros((CHANS - quant - 2, rows), jnp.float32)], axis=0
    )
    words = line_ref[...].T
    for z in range(spread):
        word = words[z * share:(z + 1) * share]
        parts = [vals, (word & (BINS - 1)).astype(jnp.float32), (word >> 7).astype(jnp.float32)]
        if total > CHANS + 2 * share:
            parts.append(jnp.zeros((total - CHANS - 2 * share, rows), jnp.float32))
        out_ref[z] = jnp.concatenate(parts, axis=0).astype(jnp.bfloat16)


def pack_kernel(quant, slots, base_ref, got_ref, out_ref, upto_ref, acc_ref):
    spread, _, rows = got_ref.shape
    groups = out_ref.shape[0]
    node_grp = TOTAL_NODES // groups
    upto_ref[...] = (
        lax.broadcasted_iota(jnp.int32, (rows, rows), 0) <= lax.broadcasted_iota(jnp.int32, (rows, rows), 1)
    ).astype(jnp.float32).astype(jnp.bfloat16)
    acc_ref[...] = jnp.zeros_like(acc_ref)
    slot = lax.broadcasted_iota(jnp.int32, (slots + TILE, rows), 0)

    def block(z, carry):
        vals = got_ref[z]
        group = got_ref[z, 0:CHANS, :].astype(jnp.float32)[quant + 1:quant + 2].astype(jnp.int32) // node_grp
        own = (lax.broadcasted_iota(jnp.int32, (groups, rows), 0) == group).astype(jnp.float32)
        run = jnp.dot(own.astype(jnp.bfloat16), upto_ref[...], preferred_element_type=jnp.float32)
        rank = jnp.sum(run * own, axis=0, keepdims=True).astype(jnp.int32) - 1
        for g in range(groups):
            base = base_ref[z * groups + g]
            start = pl.multiple_of(base // TILE * TILE, TILE)
            pick = (slot == jnp.where(group == g, rank + (base - start), -1)).astype(jnp.float32).astype(jnp.bfloat16)
            acc_ref[g, :, pl.ds(start, slots + TILE)] += lax.dot_general(
                vals, pick, NT, preferred_element_type=jnp.float32
            )
        return carry

    lax.fori_loop(0, spread, block, 0)
    out_ref[...] = acc_ref[:, :, :out_ref.shape[2]].astype(jnp.bfloat16)


def gain_kernel(quant, count_ref, chan_ref, out_ref, list_ref, left_ref, tile_ref, acc_ref):
    groups, _, slots = chan_ref.shape
    node_grp, words = out_ref.shape[0], out_ref.shape[1] // 2
    per = slots // TILE

    def fill(src, used):
        tiles = (count_ref[src] + TILE - 1) // TILE

        def put(s, used):
            list_ref[used] = src * per + s
            return used + 1

        return lax.fori_loop(0, tiles, put, used)

    used = lax.fori_loop(0, groups, fill, jnp.int32(0))
    for u in range(STEP):
        list_ref[used + u] = -1
    acc_ref[...] = jnp.zeros_like(acc_ref)
    kinds = lax.broadcasted_iota(jnp.int32, (node_grp, TILE), 0)
    level = lax.broadcasted_iota(jnp.int32, (BINS, STEP * TILE), 0).astype(jnp.float32).astype(jnp.bfloat16)

    def step(j, carry):
        for u in range(STEP):
            entry = list_ref[j * STEP + u]
            tile = jnp.maximum(entry, 0)
            src = tile // per
            at = pl.ds(pl.multiple_of(tile % per * TILE, TILE), TILE)
            part = chan_ref[src, 0:CHANS, at].astype(jnp.float32)
            kind = jnp.bitwise_and(part[quant + 1:quant + 2].astype(jnp.int32), node_grp - 1)
            mask = jnp.where((kind == kinds) & (entry >= 0), 1.0, 0.0)
            for c in range(quant + 1):
                left_ref[c * node_grp:(c + 1) * node_grp, u * TILE:(u + 1) * TILE] = part[c:c + 1] * mask
            tile_ref[u] = chan_ref[src, CHANS:, at].astype(jnp.float32)
        left = left_ref[...].astype(jnp.bfloat16)

        def feature(w, carry):
            sides = []
            for at in (w, words + w):
                digit = jnp.concatenate([tile_ref[u, pl.ds(at, 1), :] for u in range(STEP)], axis=1)
                digit = jnp.broadcast_to(digit, (16, STEP * TILE)).astype(jnp.bfloat16)
                digit = jnp.broadcast_to(digit[None], (BINS // 16, 16, STEP * TILE)).reshape(BINS, STEP * TILE)
                sides.append(jnp.where(level >= digit, jnp.bfloat16(1), jnp.bfloat16(0)))
            side = jnp.concatenate(sides, axis=0)
            acc_ref[w] += lax.dot_general(left, side, NT, preferred_element_type=jnp.float32)
            return carry

        return lax.fori_loop(0, words, feature, carry, unroll=2)

    lax.fori_loop(0, (used + STEP - 1) // STEP, step, 0)

    lane = lax.broadcasted_iota(jnp.int32, out_ref.shape, 1)
    bins = lax.broadcasted_iota(jnp.int32, (node_grp, BINS), 1)

    def best_of(w, best):
        for c in range(2):
            sums = acc_ref[w, :, c * BINS:(c + 1) * BINS]
            hess = sums[quant * node_grp:]
            hess_all = hess[:, BINS - 1:]
            sq_left = sq_right = sq_all = 0.0
            for q in range(quant):
                grad = sums[q * node_grp:(q + 1) * node_grp]
                grad_all = grad[:, BINS - 1:]
                sq_left += grad * grad
                sq_right += (grad_all - grad) * (grad_all - grad)
                sq_all += grad_all * grad_all
            score = sq_left / (hess + RIDGE) + sq_right / (hess_all - hess + RIDGE) - sq_all / (hess_all + RIDGE)
            score = jnp.where(bins < BINS - 1, score, -jnp.inf)
            top = jnp.max(score, axis=1, keepdims=True) / quant
            best = jnp.where(lane == 2 * w + c, top, best)
        return best

    out_ref[...] = lax.fori_loop(0, words, best_of, jnp.zeros(out_ref.shape, jnp.float32))


def on_device(codes, sample_idx, node_of_row, small_flag, preds, targets):
    groups = lax.axis_size("nodes")
    spread = lax.axis_size("rows")
    quant, rows = preds.shape
    node_grp = TOTAL_NODES // groups
    slots = CAP * node_grp
    width = spread * slots
    share = codes.shape[1] // spread
    digits = -(-2 * share // 16) * 16
    total = CHANS + digits

    def line(x):
        return x.reshape(1, rows)

    lines = codes.at[sample_idx].get(mode="promise_in_bounds")
    ready = pl.pallas_call(
        send_kernel,
        out_shape=jax.ShapeDtypeStruct((spread, total, rows), jnp.bfloat16),
        in_specs=[VMEM] * 5,
        out_specs=VMEM,
        compiler_params=pltpu.CompilerParams(vmem_limit_bytes=40 << 20),
    )(preds, line(targets), line(small_flag), line(node_of_row), lines)
    blocks = lax.all_to_all(ready, "rows", split_axis=0, concat_axis=0, tiled=True)
    group = blocks[:, quant + 1, :].astype(jnp.int32) // node_grp
    sizes = jnp.sum((group[:, None, :] == jnp.arange(groups, dtype=jnp.int32)[None, :, None]).astype(jnp.int32), axis=-1)
    before = jnp.arange(spread)[:, None] > jnp.arange(spread)[None, :]
    base = jnp.sum(jnp.where(before[:, :, None], sizes[None], 0), axis=1).reshape(-1)
    packed = pl.pallas_call(
        functools.partial(pack_kernel, quant, slots),
        out_shape=jax.ShapeDtypeStruct((groups, total, width), jnp.bfloat16),
        in_specs=[SMEM, VMEM],
        out_specs=VMEM,
        scratch_shapes=[
            pltpu.VMEM((rows, rows), jnp.bfloat16),
            pltpu.VMEM((groups, total, width + TILE), jnp.float32),
        ],
        compiler_params=pltpu.CompilerParams(vmem_limit_bytes=58 << 20),
    )(base, blocks)
    got = lax.all_to_all(packed, "nodes", split_axis=0, concat_axis=0, tiled=True)
    count = jnp.sum((got[:, quant, :] > 0).astype(jnp.int32), axis=-1)
    return pl.pallas_call(
        functools.partial(gain_kernel, quant),
        out_shape=jax.ShapeDtypeStruct((node_grp, 2 * share), jnp.float32),
        in_specs=[SMEM, VMEM],
        out_specs=VMEM,
        scratch_shapes=[
            pltpu.SMEM((groups * width // TILE + 2 * STEP,), jnp.int32),
            pltpu.VMEM(((quant + 1) * node_grp, STEP * TILE), jnp.float32),
            pltpu.VMEM((STEP, digits, TILE), jnp.float32),
            pltpu.VMEM((share, (quant + 1) * node_grp, 2 * BINS), jnp.float32),
        ],
        compiler_params=pltpu.CompilerParams(vmem_limit_bytes=48 << 20),
    )(count, got)


def solution(mesh):
    return jax.shard_map(
        on_device,
        mesh=mesh,
        in_specs=(
            P("rows", None),
            P(("rows", "nodes")),
            P(("rows", "nodes"), None),
            P(("rows", "nodes")),
            P(None, ("rows", "nodes")),
            P(("rows", "nodes")),
        ),
        out_specs=P("nodes", "rows"),
        check_vma=False,
    )
```

```python
import functools
import math

import jax
import jax.numpy as jnp
from jax import lax
from jax.experimental import pallas as pl
from jax.experimental.pallas import tpu as pltpu
from jax.sharding import PartitionSpec as P

BINS = 128
CAP = 48
TOTAL_NODES = 64
SMOOTH = 0.5
RIDGE = 1.0
BOOST = 8.0
CHANS = 32
TILE = 128
STEP = 8
PART = 256
NT = (((1,), (1,)), ((), ()))
VMEM = pl.BlockSpec(memory_space=pltpu.VMEM)
SMEM = pl.BlockSpec(memory_space=pltpu.SMEM)


def send_kernel(preds_ref, targets_ref, flag_ref, node_ref, line_ref, out_ref):
    quant, rows = preds_ref.shape
    spread, total, _ = out_ref.shape
    share = line_ref.shape[1] // spread
    levels = (lax.broadcasted_iota(jnp.int32, (quant, 1), 0).astype(jnp.float32) + 0.5) / quant
    weight = 1.0 + (BOOST - 1.0) * flag_ref[...].astype(jnp.float32)
    gap = (preds_ref[...].astype(jnp.float32) - targets_ref[...]) / SMOOTH
    slopes = (1.0 / (1.0 + jnp.exp(-gap)) - levels) * weight
    vals = jnp.concatenate(
        [slopes, weight, node_ref[...].astype(jnp.float32), jnp.zeros((CHANS - quant - 2, rows), jnp.float32)], axis=0
    )
    words = line_ref[...].T
    for z in range(spread):
        word = words[z * share:(z + 1) * share]
        parts = [vals, (word & (BINS - 1)).astype(jnp.float32), (word >> 7).astype(jnp.float32)]
        if total > CHANS + 2 * share:
            parts.append(jnp.zeros((total - CHANS - 2 * share, rows), jnp.float32))
        out_ref[z] = jnp.concatenate(parts, axis=0).astype(jnp.bfloat16)


def pack_kernel(quant, slots, base_ref, size_ref, got_ref, out_ref, upto_ref, acc_ref):
    spread, _, rows = got_ref.shape
    groups = out_ref.shape[0]
    node_grp = TOTAL_NODES // groups
    upto_ref[...] = (
        lax.broadcasted_iota(jnp.int32, (rows, rows), 0) <= lax.broadcasted_iota(jnp.int32, (rows, rows), 1)
    ).astype(jnp.float32).astype(jnp.bfloat16)
    acc_ref[...] = jnp.zeros_like(acc_ref)
    slot = lax.broadcasted_iota(jnp.int32, (PART, rows), 0)

    def block(z, carry):
        vals = got_ref[z]
        group = got_ref[z, 0:CHANS, :].astype(jnp.float32)[quant + 1:quant + 2].astype(jnp.int32) // node_grp
        own = (lax.broadcasted_iota(jnp.int32, (groups, rows), 0) == group).astype(jnp.float32)
        run = jnp.dot(own.astype(jnp.bfloat16), upto_ref[...], preferred_element_type=jnp.float32)
        rank = jnp.sum(run * own, axis=0, keepdims=True).astype(jnp.int32) - 1
        for g in range(groups):
            base = base_ref[z * groups + g]
            start = pl.multiple_of(base // TILE * TILE, TILE)
            end = base - start + size_ref[z * groups + g]
            rank_in = jnp.where(group == g, rank + (base - start), -1)
            for at in range(0, slots + TILE, PART):

                @pl.when(end > at)
                def _(at=at, g=g, start=start, rank_in=rank_in):
                    pick = (slot == rank_in - at).astype(jnp.float32).astype(jnp.bfloat16)
                    window = pl.ds(pl.multiple_of(start + at, TILE), PART)
                    acc_ref[g, :, window] += lax.dot_general(vals, pick, NT, preferred_element_type=jnp.float32)

        return carry

    lax.fori_loop(0, spread, block, 0)
    out_ref[...] = acc_ref[:, :, :out_ref.shape[2]].astype(jnp.bfloat16)


def gain_kernel(quant, count_ref, chan_ref, out_ref, list_ref, left_ref, tile_ref, acc_ref):
    groups, _, slots = chan_ref.shape
    node_grp, words = out_ref.shape[0], out_ref.shape[1] // 2
    per = slots // TILE

    def fill(src, used):
        tiles = (count_ref[src] + TILE - 1) // TILE

        def put(s, used):
            list_ref[used] = src * per + s
            return used + 1

        return lax.fori_loop(0, tiles, put, used)

    used = lax.fori_loop(0, groups, fill, jnp.int32(0))
    for u in range(STEP):
        list_ref[used + u] = -1
    acc_ref[...] = jnp.zeros_like(acc_ref)
    kinds = lax.broadcasted_iota(jnp.int32, (node_grp, TILE), 0)
    level = lax.broadcasted_iota(jnp.int32, (BINS, STEP * TILE), 0).astype(jnp.float32).astype(jnp.bfloat16)

    def step(j, carry):
        for u in range(STEP):
            entry = list_ref[j * STEP + u]
            tile = jnp.maximum(entry, 0)
            src = tile // per
            at = pl.ds(pl.multiple_of(tile % per * TILE, TILE), TILE)
            part = chan_ref[src, 0:CHANS, at].astype(jnp.float32)
            kind = jnp.bitwise_and(part[quant + 1:quant + 2].astype(jnp.int32), node_grp - 1)
            mask = jnp.where((kind == kinds) & (entry >= 0), 1.0, 0.0)
            for c in range(quant + 1):
                left_ref[c * node_grp:(c + 1) * node_grp, u * TILE:(u + 1) * TILE] = part[c:c + 1] * mask
            tile_ref[u] = chan_ref[src, CHANS:, at].astype(jnp.float32)
        left = left_ref[...].T.astype(jnp.bfloat16)

        def feature(w, carry):
            sides = []
            for at in (w, words + w):
                digit = jnp.concatenate([tile_ref[u, pl.ds(at, 1), :] for u in range(STEP)], axis=1)
                digit = jnp.broadcast_to(digit, (16, STEP * TILE)).astype(jnp.bfloat16)
                digit = jnp.broadcast_to(digit[None], (BINS // 16, 16, STEP * TILE)).reshape(BINS, STEP * TILE)
                sides.append(jnp.where(level >= digit, jnp.bfloat16(1), jnp.bfloat16(0)))
            side = jnp.concatenate(sides, axis=0)
            acc_ref[w] += jnp.dot(side, left, preferred_element_type=jnp.float32)
            return carry

        return lax.fori_loop(0, words, feature, carry, unroll=math.gcd(words, 16))

    lax.fori_loop(0, (used + STEP - 1) // STEP, step, 0)

    lane = lax.broadcasted_iota(jnp.int32, out_ref.shape, 1)
    bins = lax.broadcasted_iota(jnp.int32, (node_grp, BINS), 1)

    def best_of(w, best):
        for c in range(2):
            sums = acc_ref[w, c * BINS:(c + 1) * BINS, :].T
            hess = sums[quant * node_grp:]
            hess_all = hess[:, BINS - 1:]
            sq_left = sq_right = sq_all = 0.0
            for q in range(quant):
                grad = sums[q * node_grp:(q + 1) * node_grp]
                grad_all = grad[:, BINS - 1:]
                sq_left += grad * grad
                sq_right += (grad_all - grad) * (grad_all - grad)
                sq_all += grad_all * grad_all
            score = sq_left / (hess + RIDGE) + sq_right / (hess_all - hess + RIDGE) - sq_all / (hess_all + RIDGE)
            score = jnp.where(bins < BINS - 1, score, -jnp.inf)
            top = jnp.max(score, axis=1, keepdims=True) / quant
            best = jnp.where(lane == 2 * w + c, top, best)
        return best

    out_ref[...] = lax.fori_loop(0, words, best_of, jnp.zeros(out_ref.shape, jnp.float32), unroll=math.gcd(words, 4))


def on_device(codes, sample_idx, node_of_row, small_flag, preds, targets):
    groups = lax.axis_size("nodes")
    spread = lax.axis_size("rows")
    quant, rows = preds.shape
    node_grp = TOTAL_NODES // groups
    slots = CAP * node_grp
    width = spread * slots
    share = codes.shape[1] // spread
    digits = -(-2 * share // 16) * 16
    total = CHANS + digits

    def line(x):
        return x.reshape(1, rows)

    lines = codes.at[sample_idx].get(mode="promise_in_bounds")
    ready = pl.pallas_call(
        send_kernel,
        out_shape=jax.ShapeDtypeStruct((spread, total, rows), jnp.bfloat16),
        in_specs=[VMEM] * 5,
        out_specs=VMEM,
        compiler_params=pltpu.CompilerParams(vmem_limit_bytes=40 << 20),
    )(preds, line(targets), line(small_flag), line(node_of_row), lines)
    blocks = lax.all_to_all(ready, "rows", split_axis=0, concat_axis=0, tiled=True)
    group = blocks[:, quant + 1, :].astype(jnp.int32) // node_grp
    sizes = jnp.sum((group[:, None, :] == jnp.arange(groups, dtype=jnp.int32)[None, :, None]).astype(jnp.int32), axis=-1)
    before = jnp.arange(spread)[:, None] > jnp.arange(spread)[None, :]
    base = jnp.sum(jnp.where(before[:, :, None], sizes[None], 0), axis=1).reshape(-1)
    packed = pl.pallas_call(
        functools.partial(pack_kernel, quant, slots),
        out_shape=jax.ShapeDtypeStruct((groups, total, width), jnp.bfloat16),
        in_specs=[SMEM, SMEM, VMEM],
        out_specs=VMEM,
        scratch_shapes=[
            pltpu.VMEM((rows, rows), jnp.bfloat16),
            pltpu.VMEM((groups, total, width + TILE), jnp.float32),
        ],
        compiler_params=pltpu.CompilerParams(vmem_limit_bytes=58 << 20),
    )(base, sizes.reshape(-1), blocks)
    got = lax.all_to_all(packed, "nodes", split_axis=0, concat_axis=0, tiled=True)
    count = jnp.sum((got[:, quant, :] > 0).astype(jnp.int32), axis=-1)
    return pl.pallas_call(
        functools.partial(gain_kernel, quant),
        out_shape=jax.ShapeDtypeStruct((node_grp, 2 * share), jnp.float32),
        in_specs=[SMEM, VMEM],
        out_specs=VMEM,
        scratch_shapes=[
            pltpu.SMEM((groups * width // TILE + 2 * STEP,), jnp.int32),
            pltpu.VMEM(((quant + 1) * node_grp, STEP * TILE), jnp.float32),
            pltpu.VMEM((STEP, digits, TILE), jnp.float32),
            pltpu.VMEM((share, 2 * BINS, (quant + 1) * node_grp), jnp.float32),
        ],
        compiler_params=pltpu.CompilerParams(vmem_limit_bytes=48 << 20),
    )(count, got)


def solution(mesh):
    return jax.shard_map(
        on_device,
        mesh=mesh,
        in_specs=(
            P("rows", None),
            P(("rows", "nodes")),
            P(("rows", "nodes"), None),
            P(("rows", "nodes")),
            P(None, ("rows", "nodes")),
            P(("rows", "nodes")),
        ),
        out_specs=P("nodes", "rows"),
        check_vma=False,
    )
```

```python
import functools
import math

import jax
import jax.numpy as jnp
from jax import lax
from jax.experimental import pallas as pl
from jax.experimental.pallas import tpu as pltpu
from jax.sharding import PartitionSpec as P

BINS = 128
CAP = 48
TOTAL_NODES = 64
SMOOTH = 0.5
RIDGE = 1.0
BOOST = 8.0
CHANS = 32
TILE = 128
STEP = 8
PART = 256
ALIGN = 16
VMEM = pl.BlockSpec(memory_space=pltpu.VMEM)
SMEM = pl.BlockSpec(memory_space=pltpu.SMEM)


def send_kernel(preds_ref, targets_ref, flag_ref, node_ref, line_ref, out_ref):
    quant, rows = preds_ref.shape
    spread, total, _ = out_ref.shape
    share = line_ref.shape[1] // spread
    levels = (lax.broadcasted_iota(jnp.int32, (quant, 1), 0).astype(jnp.float32) + 0.5) / quant
    weight = 1.0 + (BOOST - 1.0) * flag_ref[...].astype(jnp.float32)
    gap = (preds_ref[...].astype(jnp.float32) - targets_ref[...]) / SMOOTH
    slopes = (1.0 / (1.0 + jnp.exp(-gap)) - levels) * weight
    vals = jnp.concatenate(
        [slopes, weight, node_ref[...].astype(jnp.float32), jnp.zeros((CHANS - quant - 2, rows), jnp.float32)], axis=0
    )
    words = line_ref[...].T
    for z in range(spread):
        word = words[z * share:(z + 1) * share]
        parts = [vals, (word & (BINS - 1)).astype(jnp.float32), (word >> 7).astype(jnp.float32)]
        if total > CHANS + 2 * share:
            parts.append(jnp.zeros((total - CHANS - 2 * share, rows), jnp.float32))
        out_ref[z] = jnp.concatenate(parts, axis=0).astype(jnp.bfloat16)


def pack_kernel(quant, slots, base_ref, size_ref, got_ref, out_ref, upto_ref, acc_ref):
    spread, _, rows = got_ref.shape
    groups = out_ref.shape[0]
    node_grp = TOTAL_NODES // groups
    upto_ref[...] = (
        lax.broadcasted_iota(jnp.int32, (rows, rows), 0) <= lax.broadcasted_iota(jnp.int32, (rows, rows), 1)
    ).astype(jnp.float32).astype(jnp.bfloat16)
    acc_ref[...] = jnp.zeros_like(acc_ref)
    slot = lax.broadcasted_iota(jnp.int32, (PART, rows), 0)

    def block(z, carry):
        vals = got_ref[z].astype(jnp.float32)
        group = vals[quant + 1:quant + 2].astype(jnp.int32) // node_grp
        vals = vals.T.astype(jnp.bfloat16)
        own = (lax.broadcasted_iota(jnp.int32, (groups, rows), 0) == group).astype(jnp.float32)
        run = jnp.dot(own.astype(jnp.bfloat16), upto_ref[...], preferred_element_type=jnp.float32)
        rank = jnp.sum(run * own, axis=0, keepdims=True).astype(jnp.int32) - 1

        def put(g, at):
            base = base_ref[z * groups + g]
            start = base // ALIGN * ALIGN
            pick = slot == jnp.where(group == g, rank + (base - start - at), -1)
            pick = pick.astype(jnp.float32).astype(jnp.bfloat16)
            window = pl.ds(pl.multiple_of(start + at, ALIGN), PART)
            added = jnp.dot(pick, vals, preferred_element_type=jnp.float32)
            acc_ref[g, window, :] = (acc_ref[g, window, :].astype(jnp.float32) + added).astype(jnp.bfloat16)

        for g in range(groups):
            put(g, 0)
        for g in range(groups):
            for at in range(PART, slots + ALIGN, PART):
                pl.when(base_ref[z * groups + g] % ALIGN + size_ref[z * groups + g] > at)(functools.partial(put, g, at))
        return carry

    lax.fori_loop(0, spread, block, 0)

    def turn(c, carry):
        window = pl.ds(pl.multiple_of(c * slots, TILE), slots)
        for g in range(groups):
            out_ref[g, :, window] = acc_ref[g, window, :].astype(jnp.float32).T.astype(jnp.bfloat16)
        return carry

    lax.fori_loop(0, spread, turn, 0)


def gain_kernel(quant, count_ref, chan_ref, out_ref, list_ref, left_ref, tile_ref, acc_ref):
    groups, _, slots = chan_ref.shape
    node_grp, words = out_ref.shape[0], out_ref.shape[1] // 2
    per = slots // TILE

    def fill(src, used):
        tiles = (count_ref[src] + TILE - 1) // TILE

        def put(s, used):
            list_ref[used] = src * per + s
            return used + 1

        return lax.fori_loop(0, tiles, put, used)

    used = lax.fori_loop(0, groups, fill, jnp.int32(0))
    for u in range(STEP):
        list_ref[used + u] = -1
    acc_ref[...] = jnp.zeros_like(acc_ref)
    kinds = lax.broadcasted_iota(jnp.int32, (node_grp, TILE), 0)
    level = lax.broadcasted_iota(jnp.int32, (BINS, STEP * TILE), 0).astype(jnp.float32).astype(jnp.bfloat16)

    def step(j, carry):
        for u in range(STEP):
            entry = list_ref[j * STEP + u]
            tile = jnp.maximum(entry, 0)
            src = tile // per
            at = pl.ds(pl.multiple_of(tile % per * TILE, TILE), TILE)
            part = chan_ref[src, 0:CHANS, at].astype(jnp.float32)
            kind = jnp.bitwise_and(part[quant + 1:quant + 2].astype(jnp.int32), node_grp - 1)
            mask = jnp.where((kind == kinds) & (entry >= 0), 1.0, 0.0)
            for c in range(quant + 1):
                left_ref[c * node_grp:(c + 1) * node_grp, u * TILE:(u + 1) * TILE] = part[c:c + 1] * mask
            tile_ref[u] = chan_ref[src, CHANS:, at].astype(jnp.float32)
        left = left_ref[...].T.astype(jnp.bfloat16)

        def feature(w, carry):
            sides = []
            for at in (w, words + w):
                digit = jnp.concatenate([tile_ref[u, pl.ds(at, 1), :] for u in range(STEP)], axis=1)
                digit = jnp.broadcast_to(digit, (16, STEP * TILE)).astype(jnp.bfloat16)
                digit = jnp.broadcast_to(digit[None], (BINS // 16, 16, STEP * TILE)).reshape(BINS, STEP * TILE)
                sides.append(jnp.where(level >= digit, jnp.bfloat16(1), jnp.bfloat16(0)))
            side = jnp.concatenate(sides, axis=0)
            acc_ref[w] += jnp.dot(side, left, preferred_element_type=jnp.float32)
            return carry

        return lax.fori_loop(0, words, feature, carry, unroll=math.gcd(words, 16))

    lax.fori_loop(0, (used + STEP - 1) // STEP, step, 0)

    lane = lax.broadcasted_iota(jnp.int32, out_ref.shape, 1)
    bins = lax.broadcasted_iota(jnp.int32, (node_grp, BINS), 1)

    def best_of(w, best):
        for c in range(2):
            sums = acc_ref[w, c * BINS:(c + 1) * BINS, :].T
            hess = sums[quant * node_grp:]
            hess_all = hess[:, BINS - 1:]
            sq_left = sq_right = sq_all = 0.0
            for q in range(quant):
                grad = sums[q * node_grp:(q + 1) * node_grp]
                grad_all = grad[:, BINS - 1:]
                sq_left += grad * grad
                sq_right += (grad_all - grad) * (grad_all - grad)
                sq_all += grad_all * grad_all
            score = sq_left / (hess + RIDGE) + sq_right / (hess_all - hess + RIDGE) - sq_all / (hess_all + RIDGE)
            score = jnp.where(bins < BINS - 1, score, -jnp.inf)
            top = jnp.max(score, axis=1, keepdims=True) / quant
            best = jnp.where(lane == 2 * w + c, top, best)
        return best

    out_ref[...] = lax.fori_loop(0, words, best_of, jnp.zeros(out_ref.shape, jnp.float32), unroll=math.gcd(words, 4))


def on_device(codes, sample_idx, node_of_row, small_flag, preds, targets):
    groups = lax.axis_size("nodes")
    spread = lax.axis_size("rows")
    quant, rows = preds.shape
    node_grp = TOTAL_NODES // groups
    slots = CAP * node_grp
    width = spread * slots
    share = codes.shape[1] // spread
    digits = -(-2 * share // 16) * 16
    total = CHANS + digits

    def line(x):
        return x.reshape(1, rows)

    lines = codes.at[sample_idx].get(mode="promise_in_bounds")
    ready = pl.pallas_call(
        send_kernel,
        out_shape=jax.ShapeDtypeStruct((spread, total, rows), jnp.bfloat16),
        in_specs=[VMEM] * 5,
        out_specs=VMEM,
        compiler_params=pltpu.CompilerParams(vmem_limit_bytes=40 << 20),
    )(preds, line(targets), line(small_flag), line(node_of_row), lines)
    blocks = lax.all_to_all(ready, "rows", split_axis=0, concat_axis=0, tiled=True)
    group = blocks[:, quant + 1, :].astype(jnp.int32) // node_grp
    sizes = jnp.sum((group[:, None, :] == jnp.arange(groups, dtype=jnp.int32)[None, :, None]).astype(jnp.int32), axis=-1)
    before = jnp.arange(spread)[:, None] > jnp.arange(spread)[None, :]
    base = jnp.sum(jnp.where(before[:, :, None], sizes[None], 0), axis=1).reshape(-1)
    packed = pl.pallas_call(
        functools.partial(pack_kernel, quant, slots),
        out_shape=jax.ShapeDtypeStruct((groups, total, width), jnp.bfloat16),
        in_specs=[SMEM, SMEM, VMEM],
        out_specs=VMEM,
        scratch_shapes=[
            pltpu.VMEM((rows, rows), jnp.bfloat16),
            pltpu.VMEM((groups, width + 2 * PART, total), jnp.bfloat16),
        ],
        compiler_params=pltpu.CompilerParams(vmem_limit_bytes=58 << 20),
    )(base, sizes.reshape(-1), blocks)
    got = lax.all_to_all(packed, "nodes", split_axis=0, concat_axis=0, tiled=True)
    count = jnp.sum((got[:, quant, :] > 0).astype(jnp.int32), axis=-1)
    return pl.pallas_call(
        functools.partial(gain_kernel, quant),
        out_shape=jax.ShapeDtypeStruct((node_grp, 2 * share), jnp.float32),
        in_specs=[SMEM, VMEM],
        out_specs=VMEM,
        scratch_shapes=[
            pltpu.SMEM((groups * width // TILE + 2 * STEP,), jnp.int32),
            pltpu.VMEM(((quant + 1) * node_grp, STEP * TILE), jnp.float32),
            pltpu.VMEM((STEP, digits, TILE), jnp.float32),
            pltpu.VMEM((share, 2 * BINS, (quant + 1) * node_grp), jnp.float32),
        ],
        compiler_params=pltpu.CompilerParams(vmem_limit_bytes=48 << 20),
    )(count, got)


def solution(mesh):
    return jax.shard_map(
        on_device,
        mesh=mesh,
        in_specs=(
            P("rows", None),
            P(("rows", "nodes")),
            P(("rows", "nodes"), None),
            P(("rows", "nodes")),
            P(None, ("rows", "nodes")),
            P(("rows", "nodes")),
        ),
        out_specs=P("nodes", "rows"),
        check_vma=False,
    )
```

```python
import functools
import math

import jax
import jax.numpy as jnp
from jax import lax
from jax.experimental import pallas as pl
from jax.experimental.pallas import tpu as pltpu
from jax.sharding import PartitionSpec as P

BINS = 128
CAP = 48
TOTAL_NODES = 64
SMOOTH = 0.5
RIDGE = 1.0
BOOST = 8.0
CHANS = 32
TILE = 128
STEP = 8
PART = 256
ALIGN = 16
VMEM = pl.BlockSpec(memory_space=pltpu.VMEM)
SMEM = pl.BlockSpec(memory_space=pltpu.SMEM)


def send_kernel(preds_ref, targets_ref, flag_ref, node_ref, line_ref, out_ref):
    quant, rows = preds_ref.shape
    spread, total, _ = out_ref.shape
    share = line_ref.shape[1] // spread
    levels = (lax.broadcasted_iota(jnp.int32, (quant, 1), 0).astype(jnp.float32) + 0.5) / quant
    weight = 1.0 + (BOOST - 1.0) * flag_ref[...].astype(jnp.float32)
    gap = (preds_ref[...].astype(jnp.float32) - targets_ref[...]) / SMOOTH
    slopes = (1.0 / (1.0 + jnp.exp(-gap)) - levels) * weight
    vals = jnp.concatenate(
        [slopes, weight, node_ref[...].astype(jnp.float32), jnp.zeros((CHANS - quant - 2, rows), jnp.float32)], axis=0
    )
    words = line_ref[...].T
    for z in range(spread):
        word = words[z * share:(z + 1) * share]
        parts = [vals, (word & (BINS - 1)).astype(jnp.float32), (word >> 7).astype(jnp.float32)]
        if total > CHANS + 2 * share:
            parts.append(jnp.zeros((total - CHANS - 2 * share, rows), jnp.float32))
        out_ref[z] = jnp.concatenate(parts, axis=0).astype(jnp.bfloat16)


def pack_kernel(quant, slots, base_ref, size_ref, got_ref, out_ref, upto_ref, acc_ref):
    spread, _, rows = got_ref.shape
    groups = out_ref.shape[0]
    node_grp = TOTAL_NODES // groups
    upto_ref[...] = (
        lax.broadcasted_iota(jnp.int32, (rows, rows), 0) <= lax.broadcasted_iota(jnp.int32, (rows, rows), 1)
    ).astype(jnp.float32).astype(jnp.bfloat16)
    acc_ref[...] = jnp.zeros_like(acc_ref)
    slot = lax.broadcasted_iota(jnp.int32, (PART, rows), 0)

    def block(z, carry):
        vals = got_ref[z].astype(jnp.float32)
        group = vals[quant + 1:quant + 2].astype(jnp.int32) // node_grp
        vals = vals.T.astype(jnp.bfloat16)
        own = (lax.broadcasted_iota(jnp.int32, (groups, rows), 0) == group).astype(jnp.float32)
        run = jnp.dot(own.astype(jnp.bfloat16), upto_ref[...], preferred_element_type=jnp.float32)
        rank = jnp.sum(run * own, axis=0, keepdims=True).astype(jnp.int32) - 1

        def put(g, at):
            base = base_ref[z * groups + g]
            start = base // ALIGN * ALIGN
            pick = slot == jnp.where(group == g, rank + (base - start - at), -1)
            pick = pick.astype(jnp.float32).astype(jnp.bfloat16)
            window = pl.ds(pl.multiple_of(start + at, ALIGN), PART)
            added = jnp.dot(pick, vals, preferred_element_type=jnp.float32)
            acc_ref[g, window, :] = (acc_ref[g, window, :].astype(jnp.float32) + added).astype(jnp.bfloat16)

        for g in range(groups):
            put(g, 0)
        for g in range(groups):
            for at in range(PART, slots + ALIGN, PART):
                pl.when(base_ref[z * groups + g] % ALIGN + size_ref[z * groups + g] > at)(functools.partial(put, g, at))
        return carry

    lax.fori_loop(0, spread, block, 0, unroll=2 - spread % 2)

    def turn(c, carry):
        window = pl.ds(pl.multiple_of(c * slots, TILE), slots)
        for g in range(groups):
            out_ref[g, :, window] = acc_ref[g, window, :].astype(jnp.float32).T.astype(jnp.bfloat16)
        return carry

    lax.fori_loop(0, spread, turn, 0)


def gain_kernel(quant, count_ref, chan_ref, out_ref, list_ref, left_ref, tile_ref, acc_ref):
    groups, _, slots = chan_ref.shape
    node_grp, words = out_ref.shape[0], out_ref.shape[1] // 2
    per = slots // TILE

    def fill(src, used):
        tiles = (count_ref[src] + TILE - 1) // TILE

        def put(s, used):
            list_ref[used] = src * per + s
            return used + 1

        return lax.fori_loop(0, tiles, put, used)

    used = lax.fori_loop(0, groups, fill, jnp.int32(0))
    for u in range(STEP):
        list_ref[used + u] = -1
    acc_ref[...] = jnp.zeros_like(acc_ref)
    kinds = lax.broadcasted_iota(jnp.int32, (node_grp, TILE), 0)
    level = lax.broadcasted_iota(jnp.int32, (BINS, STEP * TILE), 0).astype(jnp.float32).astype(jnp.bfloat16)

    def step(j, carry):
        for u in range(STEP):
            entry = list_ref[j * STEP + u]
            tile = jnp.maximum(entry, 0)
            src = tile // per
            at = pl.ds(pl.multiple_of(tile % per * TILE, TILE), TILE)
            part = chan_ref[src, 0:CHANS, at].astype(jnp.float32)
            kind = jnp.bitwise_and(part[quant + 1:quant + 2].astype(jnp.int32), node_grp - 1)
            mask = jnp.where((kind == kinds) & (entry >= 0), 1.0, 0.0)
            for c in range(quant + 1):
                left_ref[c * node_grp:(c + 1) * node_grp, u * TILE:(u + 1) * TILE] = part[c:c + 1] * mask
            tile_ref[u] = chan_ref[src, CHANS:, at].astype(jnp.float32)
        left = left_ref[...].T.astype(jnp.bfloat16)

        def feature(w, carry):
            sides = []
            for at in (w, words + w):
                digit = jnp.concatenate([tile_ref[u, pl.ds(at, 1), :] for u in range(STEP)], axis=1)
                digit = jnp.broadcast_to(digit, (16, STEP * TILE)).astype(jnp.bfloat16)
                digit = jnp.broadcast_to(digit[None], (BINS // 16, 16, STEP * TILE)).reshape(BINS, STEP * TILE)
                sides.append(jnp.where(level >= digit, jnp.bfloat16(1), jnp.bfloat16(0)))
            side = jnp.concatenate(sides, axis=0)
            acc_ref[w] += jnp.dot(side, left, preferred_element_type=jnp.float32)
            return carry

        return lax.fori_loop(0, words, feature, carry, unroll=math.gcd(words, 16))

    lax.fori_loop(0, (used + STEP - 1) // STEP, step, 0)

    lane = lax.broadcasted_iota(jnp.int32, out_ref.shape, 1)
    bins = lax.broadcasted_iota(jnp.int32, (node_grp, BINS), 1)

    def best_of(w, best):
        for c in range(2):
            sums = acc_ref[w, c * BINS:(c + 1) * BINS, :].T
            hess = sums[quant * node_grp:]
            hess_all = hess[:, BINS - 1:]
            sq_left = sq_right = sq_all = 0.0
            for q in range(quant):
                grad = sums[q * node_grp:(q + 1) * node_grp]
                grad_all = grad[:, BINS - 1:]
                sq_left += grad * grad
                sq_right += (grad_all - grad) * (grad_all - grad)
                sq_all += grad_all * grad_all
            score = sq_left / (hess + RIDGE) + sq_right / (hess_all - hess + RIDGE) - sq_all / (hess_all + RIDGE)
            score = jnp.where(bins < BINS - 1, score, -jnp.inf)
            top = jnp.max(score, axis=1, keepdims=True) / quant
            best = jnp.where(lane == 2 * w + c, top, best)
        return best

    out_ref[...] = lax.fori_loop(0, words, best_of, jnp.zeros(out_ref.shape, jnp.float32), unroll=math.gcd(words, 4))


def on_device(codes, sample_idx, node_of_row, small_flag, preds, targets):
    groups = lax.axis_size("nodes")
    spread = lax.axis_size("rows")
    quant, rows = preds.shape
    node_grp = TOTAL_NODES // groups
    slots = CAP * node_grp
    width = spread * slots
    share = codes.shape[1] // spread
    digits = -(-2 * share // 16) * 16
    total = CHANS + digits

    def line(x):
        return x.reshape(1, rows)

    lines = codes.at[sample_idx].get(mode="promise_in_bounds")
    ready = pl.pallas_call(
        send_kernel,
        out_shape=jax.ShapeDtypeStruct((spread, total, rows), jnp.bfloat16),
        in_specs=[VMEM] * 5,
        out_specs=VMEM,
        compiler_params=pltpu.CompilerParams(vmem_limit_bytes=40 << 20),
    )(preds, line(targets), line(small_flag), line(node_of_row), lines)
    blocks = lax.all_to_all(ready, "rows", split_axis=0, concat_axis=0, tiled=True)
    group = blocks[:, quant + 1, :].astype(jnp.int32) // node_grp
    sizes = jnp.sum((group[:, None, :] == jnp.arange(groups, dtype=jnp.int32)[None, :, None]).astype(jnp.int32), axis=-1)
    before = jnp.arange(spread)[:, None] > jnp.arange(spread)[None, :]
    base = jnp.sum(jnp.where(before[:, :, None], sizes[None], 0), axis=1).reshape(-1)
    packed = pl.pallas_call(
        functools.partial(pack_kernel, quant, slots),
        out_shape=jax.ShapeDtypeStruct((groups, total, width), jnp.bfloat16),
        in_specs=[SMEM, SMEM, VMEM],
        out_specs=VMEM,
        scratch_shapes=[
            pltpu.VMEM((rows, rows), jnp.bfloat16),
            pltpu.VMEM((groups, width + 2 * PART, total), jnp.bfloat16),
        ],
        compiler_params=pltpu.CompilerParams(vmem_limit_bytes=58 << 20),
    )(base, sizes.reshape(-1), blocks)
    got = lax.all_to_all(packed, "nodes", split_axis=0, concat_axis=0, tiled=True)
    count = jnp.sum((got[:, quant, :] > 0).astype(jnp.int32), axis=-1)
    return pl.pallas_call(
        functools.partial(gain_kernel, quant),
        out_shape=jax.ShapeDtypeStruct((node_grp, 2 * share), jnp.float32),
        in_specs=[SMEM, VMEM],
        out_specs=VMEM,
        scratch_shapes=[
            pltpu.SMEM((groups * width // TILE + 2 * STEP,), jnp.int32),
            pltpu.VMEM(((quant + 1) * node_grp, STEP * TILE), jnp.float32),
            pltpu.VMEM((STEP, digits, TILE), jnp.float32),
            pltpu.VMEM((share, 2 * BINS, (quant + 1) * node_grp), jnp.float32),
        ],
        compiler_params=pltpu.CompilerParams(vmem_limit_bytes=48 << 20),
    )(count, got)


def solution(mesh):
    return jax.shard_map(
        on_device,
        mesh=mesh,
        in_specs=(
            P("rows", None),
            P(("rows", "nodes")),
            P(("rows", "nodes"), None),
            P(("rows", "nodes")),
            P(None, ("rows", "nodes")),
            P(("rows", "nodes")),
        ),
        out_specs=P("nodes", "rows"),
        check_vma=False,
    )
```
